32 devices in a mesh: grp: 4 (over z), ep: 8 (over y, x, core).
Axes of the slice: x: 2, y: 2, z: 4, core: 2. Of those that a mesh axis runs over, the one named last changes fastest.
Arguments:
- tokens: bfloat16 [4096, 2048], P(('grp', 'ep')), may hold values from -6 to 6
- norm_gain: float32 [2048], replicated, may hold values from 0.25 to 1.75
- w_gate: bfloat16 [8, 2048, 512], P('ep', 'grp'), may hold values from -0.125 to 0.125
- w_up: bfloat16 [8, 2048, 512], P('ep', 'grp'), may hold values from -0.125 to 0.125
- w_down: bfloat16 [8, 512, 2048], P('ep', None, 'grp'), may hold values from -0.25 to 0.25
- expert_ids: int32 [4096, 2], P(('grp', 'ep')), may hold values from 0 to 7, all different within a row; in each aligned block of 128 rows (0 to 127, 128 to 255, ...) at most 48 rows name the same one
- probs: float32 [4096, 2], P(('grp', 'ep')), may hold values from 0.1 to 1
- out_grad: bfloat16 [4096, 2048], P(('grp', 'ep')), may hold values from -6 to 6
Outputs:
- grad_tokens: bfloat16 [4096, 2048], P(('grp', 'ep'))
- grad_up: float32 [8, 2048, 512], P('ep', 'grp')
- grad_down: float32 [8, 512, 2048], P('ep', None, 'grp')
The draws below stay inside these ranges and needn't reach their ends.
Inputs may be any that keep to these rules, and one draw needn't show every extreme that they name: `expert_ids`: each row names 2 different experts; among the 128 rows of one device, no expert is named by more than 48 rows, a bound that some block reaches.
All inputs are finite; a program needn't handle non-finite values.
Results may differ from the reference program's by a relative error of at most 0.017.
Values may be sent and summed in bfloat16 or wider, within the bound.
A program may use at most 64 MiB of HBM per device.

```python
import math
import jax
import jax.numpy as jnp
import numpy as np
from jax import lax

D = 2048
F = 512
K = 2
TOK_DEV = 128
EXPERTS = 8
CAP = 48
TOKENS = 4096
N_GRP = 4
N_EP = 8


def levels(stream_key, shape, pieces, least, largest):
    level, own = 1.0, jax.random.fold_in(stream_key, 6)
    for position, shards_of in pieces:
        draws = jnp.exp(jax.random.uniform(jax.random.fold_in(own, position), (shards_of,), jnp.float32, least / len(pieces), largest / len(pieces)))
        level = level * jnp.repeat(draws, shape[position] // shards_of).reshape([-1 if axis == position else 1 for axis in range(len(shape))])
    return level


def shared_out(own_key, own, number, rows, amount, top, most, lean):
    sequence = jax.random.permutation(own_key, amount)
    heavy_load, common = shares(amount, rows * top, most, lean, True), shares(amount, rows * top, most, lean, False)
    places = jnp.arange(amount)

    def named(lengths, turn):
        used = int((lengths > 0).sum())
        fixed = max(1, used // 4)
        shifted = fixed + (places - fixed + turn * (used - fixed)) % max(1, amount - fixed)
        return jnp.zeros((amount,), jnp.int32).at[sequence[jnp.where(places < fixed, places, shifted)]].set(jnp.asarray(lengths, jnp.int32))

    lengths = jnp.where(number % 4 == 0, named(heavy_load, number // 4), named(common, number - number // 4 - 1))
    mixed = jax.random.permutation(jax.random.fold_in(own, 3), amount)
    giver, receiver = mixed[0:amount // 2 * 2:2], mixed[1:amount // 2 * 2:2]
    margin = jnp.minimum(lengths[giver] - 1, most - lengths[receiver]) // 2
    margin = jnp.where((giver == sequence[0]) | (receiver == sequence[0]) | (lengths[receiver] == 0), 0, jnp.maximum(margin, 0))
    shifted = jax.random.randint(jax.random.fold_in(own, 4), (amount // 2,), 0, 1 << 20) % (margin + 1)
    lengths = lengths.at[giver].add(-shifted).at[receiver].add(shifted)
    labels = jnp.searchsorted(jnp.cumsum(lengths), jnp.arange(rows * top), side="right").astype(jnp.int32)
    listing = labels.reshape(top, rows).T
    listing = listing[jax.random.permutation(jax.random.fold_in(own, 1), rows)]
    turn = jax.random.randint(jax.random.fold_in(own, 2), (rows, 1), 0, top)
    return jnp.take_along_axis(listing, (jnp.arange(top)[None, :] + turn) % top, axis=1)


def shares(amount, total, reach, slope, full):
    loads = [(1 << 20) // math.isqrt(standing ** slope) + 1 for standing in range(1, amount + 1)]
    largest = reach if full else min(reach, max(-(-total // amount), total * loads[0] // sum(loads)))
    least = 1 if total - largest >= amount - 1 else 0
    given, spare = [largest] + [least] * (amount - 1), total - largest - least * (amount - 1)
    while spare > 0:
        free = [i for i in range(1, amount) if given[i] < largest] or [i for i in range(1, amount) if given[i] < reach]
        mass, budget = sum([loads[i] for i in free]), spare
        for i in free:
            addition = min(reach - given[i], max(1, budget * loads[i] // mass), spare)
            given[i] = given[i] + addition
            spare = spare - addition
    return np.array(given)


def scatter_about(key, shape, spread, bound, shards=(), kind=jnp.bfloat16):
    loudness = levels(key, shape, shards, -0.22, 0.18) if shards else 1.0
    drawn = jax.random.normal(key, shape, jnp.float32) * spread * loudness
    return jnp.minimum(jnp.maximum(drawn, -bound), bound).astype(kind)


def setup_inputs(seed: int = 0) -> dict:
    arg_keys = jax.random.split(jax.random.key(seed), 9)
    tokens = scatter_about(arg_keys[0], (TOKENS, D), 1.0, 6.0, ((0, 32),))
    norm_gain = jnp.clip(1.0 + 0.15 * jax.random.normal(arg_keys[1], (D,), jnp.float32), 0.25, 1.75)
    w_gate = scatter_about(arg_keys[2], (EXPERTS, D, F), D ** -0.5, 0.125, ((0, 8), (1, 4)))
    w_up = scatter_about(arg_keys[3], (EXPERTS, D, F), D ** -0.5, 0.125, ((0, 8), (1, 4)))
    w_down = scatter_about(arg_keys[4], (EXPERTS, F, D), F ** -0.5, 0.25, ((0, 8), (2, 4)))
    expert_ids_keys = jax.random.split(jax.random.fold_in(arg_keys[5], 1), TOKENS // TOK_DEV)
    expert_ids_turns = jax.random.permutation(jax.random.fold_in(arg_keys[5], 3), TOKENS // TOK_DEV)
    expert_ids = jax.vmap(lambda own, number: shared_out(jax.random.fold_in(arg_keys[5], 2), own, number, TOK_DEV, EXPERTS, K, CAP, 2))(expert_ids_keys, expert_ids_turns).reshape((TOKENS, K))
    probs = jnp.clip(jnp.exp(math.log(1.0) - 2.3025851 * jax.random.uniform(arg_keys[6], (TOKENS, K), jnp.float32) ** levels(arg_keys[6], (TOKENS, K), ((0, 32),), -0.2, 0.2)), 0.1, 1.0)
    out_grad = scatter_about(arg_keys[7], (TOKENS, D), 1.0, 6.0, ((0, 32),))
    return {"tokens": tokens, "norm_gain": norm_gain, "w_gate": w_gate, "w_up": w_up, "w_down": w_down, "expert_ids": expert_ids, "probs": probs, "out_grad": out_grad}


EPS = 1e-06

def expert_pass(hidden_rows, cot_rows, gate_full, up_full, down_full):
    hidden_f = hidden_rows.astype(jnp.float32)
    cot_f = cot_rows.astype(jnp.float32)
    gate_f = gate_full.astype(jnp.float32)
    up_f = up_full.astype(jnp.float32)
    pre_gate = jnp.dot(hidden_f, gate_f)
    pre_up = jnp.dot(hidden_f, up_f)
    sigmoid_gate = jax.nn.sigmoid(pre_gate)
    act_gate = pre_gate * sigmoid_gate
    swiglu = (act_gate * pre_up).astype(jnp.bfloat16)
    d_swiglu = jnp.dot(cot_f, down_full.astype(jnp.float32).T)
    d_up_pre = (d_swiglu * act_gate).astype(jnp.bfloat16)
    d_gate_pre = (d_swiglu * pre_up * sigmoid_gate * (1.0 + pre_gate * (1.0 - sigmoid_gate))).astype(jnp.bfloat16)
    d_hidden = (jnp.dot(d_gate_pre.astype(jnp.float32), gate_f.T) + jnp.dot(d_up_pre.astype(jnp.float32), up_f.T)).astype(jnp.bfloat16)
    part_up = jnp.dot(hidden_f.T, d_up_pre.astype(jnp.float32))
    part_down = jnp.dot(swiglu.astype(jnp.float32).T, cot_f)
    return (d_hidden, part_up, part_down)

def reference(tokens, norm_gain, w_gate, w_up, w_down, expert_ids, probs, out_grad):
    token_f = tokens.astype(jnp.float32)
    inverse = lax.rsqrt(lax.optimization_barrier(jnp.mean(token_f * token_f, axis=1, keepdims=True)) + EPS)
    normed = token_f * inverse
    hidden = (normed * norm_gain[None, :]).astype(jnp.bfloat16)
    cot_full = out_grad.astype(jnp.float32)
    top_count = expert_ids.shape[1]
    group_rows = N_EP * TOK_DEV
    slot_count = N_EP * CAP
    width = tokens.shape[1]

    def per_expert(d_normed, expert):
        gate_full = w_gate[expert]
        up_full = w_up[expert]
        down_full = w_down[expert]

        def per_group(carry, group):
            d_acc, sum_up, sum_down = carry
            start = (group * group_rows).astype(jnp.int32)
            ids_group = lax.dynamic_slice_in_dim(expert_ids, start, group_rows, 0).reshape(-1)
            match = ids_group == expert
            flat_index = jnp.nonzero(match, size=slot_count, fill_value=0)[0].astype(jnp.int32)
            count = jnp.sum(match.astype(jnp.int32))
            valid = jnp.arange(slot_count, dtype=jnp.int32) < count
            global_row = start + flat_index // top_count
            which = flat_index % top_count
            hidden_rows = jnp.where(valid[:, None], hidden[global_row], jnp.zeros((), jnp.bfloat16)).astype(jnp.bfloat16)
            weight_rows = probs[global_row, which]
            cot_rows = (weight_rows[:, None] * cot_full[global_row]).astype(jnp.bfloat16)
            cot_rows = jnp.where(valid[:, None], cot_rows, jnp.zeros((), jnp.bfloat16)).astype(jnp.bfloat16)
            d_hidden, part_up, part_down = expert_pass(hidden_rows, cot_rows, gate_full, up_full, down_full)
            added = jnp.where(valid[:, None], d_hidden.astype(jnp.float32), jnp.zeros((), jnp.float32))
            d_acc = d_acc.at[global_row].add(added)
            sum_up = sum_up + lax.optimization_barrier(part_up.astype(jnp.bfloat16)).astype(jnp.float32)
            sum_down = sum_down + lax.optimization_barrier(part_down.astype(jnp.bfloat16)).astype(jnp.float32)
            return ((d_acc, sum_up, sum_down), None)
        first = (d_normed, jnp.zeros((width, F), jnp.float32), jnp.zeros((F, width), jnp.float32))
        (d_normed, sum_up, sum_down), _ = lax.scan(per_group, first, jnp.arange(N_GRP, dtype=jnp.int32))
        return (d_normed, (sum_up, sum_down))
    d_start = jnp.zeros(tokens.shape, jnp.float32)
    d_normed, (all_up, all_down) = lax.scan(per_expert, d_start, jnp.arange(EXPERTS, dtype=jnp.int32))
    factor = 1.0 / math.sqrt(TOKENS * top_count / EXPERTS)
    d_scaled = d_normed * norm_gain[None, :]
    dot_mean = lax.optimization_barrier(jnp.mean(d_scaled * normed, axis=1, keepdims=True))
    grad_tokens = (inverse * (d_scaled - normed * dot_mean)).astype(jnp.bfloat16)
    return (grad_tokens, all_up * factor, all_down * factor)
```

```python
import functools
import math

import jax
import jax.numpy as jnp
from jax import lax
from jax.experimental import pallas as pl
from jax.experimental.pallas import tpu as pltpu
from jax.sharding import PartitionSpec as P

EPS = 1e-06
F32 = jnp.float32
BF16 = jnp.bfloat16


def dot(a, b, ca, cb):
    return lax.dot_general(a, b, (((ca,), (cb,)), ((), ())), preferred_element_type=F32)


def kernel(
    grp_n, ep_n, slots_each, chunks, factor,
    tok, gain, wg, wu, wd, ids, probs, cot_in,
    gt, gu, gd,
    wgu_all, wd_all, h_send, c_send, h_recv, c_recv, d_send, d_recv,
    gates, ups, normed_s, inv_s, pick_s, own_up, own_down, left_up, left_down, right_up, right_down,
    ag_send, ag_recv, rs_send, rs_recv, h_ss, h_rs, c_ss, c_rs, d_ss, d_rs,
):
    g, me = lax.axis_index("grp"), lax.axis_index("ep")
    rows, width = tok.shape
    deep = width // grp_n
    fc = wg.shape[1] // chunks
    slots = ep_n * slots_each
    last = grp_n - 1
    right, left = lax.rem(g + 1, grp_n), lax.rem(g + grp_n - 1, grp_n)

    barrier = pltpu.get_barrier_semaphore()

    def greet(e_id, g_id):
        pl.semaphore_signal(
            barrier, inc=1, device_id=(g_id, e_id), device_id_type=pl.DeviceIdType.MESH
        )

    for d in range(1, ep_n):
        greet(lax.rem(me + d, ep_n), g)
    pl.when(g < last)(lambda: greet(me, right))
    pl.when(g > 0)(lambda: greet(me, left))
    beside = (g < last).astype(jnp.int32) + (g > 0).astype(jnp.int32)
    pl.semaphore_wait(barrier, ep_n - 1 + beside)

    def remote(src, dst, ss, rs, g_id, e_id):
        return pltpu.make_async_remote_copy(
            src_ref=src, dst_ref=dst, send_sem=ss, recv_sem=rs,
            device_id=(g_id, e_id), device_id_type=pl.DeviceIdType.MESH,
        )

    def weight_copies(c, j, way):
        to = left if way else right
        return [
            remote(buf.at[c, j], buf.at[c, j], ag_send.at[way, c, j, m], ag_recv.at[c, j, m], to, me)
            for m, buf in enumerate((wgu_all, wd_all))
        ]

    def go(copies):
        for copy in copies:
            copy.start()

    def landed(copies):
        for copy in copies:
            copy.wait_recv()

    def gone(copies):
        for copy in copies:
            copy.wait_send()

    def own_shard(c):
        pl.when(g < last)(lambda: go(weight_copies(c, g, 0)))
        pl.when(g > 0)(lambda: go(weight_copies(c, g, 1)))

    for c in range(chunks):
        cols = slice(c * fc, (c + 1) * fc)
        wgu_all[c, g, 0] = wg[:, cols]
        wgu_all[c, g, 1] = wu[:, cols]
        wd_all[c, g] = wd[cols, :]
        if c < 2:
            own_shard(c)

    id0, id1 = ids[0:1, :], ids[1:2, :]
    experts = lax.broadcasted_iota(jnp.int32, (ep_n, rows), 0)
    hit0, hit1 = (experts == id0).astype(F32), (experts == id1).astype(F32)
    before = lax.broadcasted_iota(jnp.int32, (rows, rows), 0) < lax.broadcasted_iota(
        jnp.int32, (rows, rows), 1
    )
    rank = dot((hit0 + hit1).astype(BF16), before.astype(F32).astype(BF16), 1, 0)
    at0 = id0 * slots_each + jnp.sum(hit0 * rank, axis=0, keepdims=True).astype(jnp.int32)
    at1 = id1 * slots_each + jnp.sum(hit1 * rank, axis=0, keepdims=True).astype(jnp.int32)
    slot = lax.broadcasted_iota(jnp.int32, (slots, rows), 0)
    pick0, pick1 = (slot == at0).astype(F32), (slot == at1).astype(F32)
    pick = (pick0 + pick1).astype(BF16)
    pick_s[...] = pick
    slot_prob = jnp.sum(pick0 * probs[0:1, :] + pick1 * probs[1:2, :], axis=1, keepdims=True)

    token_f = tok[...].astype(F32)
    inverse = lax.rsqrt(jnp.mean(token_f * token_f, axis=1, keepdims=True) + EPS)
    inv_s[...] = jnp.broadcast_to(inverse, inv_s.shape)
    for j in range(grp_n):
        cols = slice(j * deep, (j + 1) * deep)
        normed = tok[:, cols].astype(F32) * inverse
        normed_s[j] = normed
        hidden = (normed * gain[:, cols]).astype(BF16)
        h_send[j] = dot(pick, hidden, 1, 0).astype(BF16)
        c_send[j] = (dot(pick, cot_in[:, cols], 1, 0) * slot_prob).astype(BF16)

    def row_slots(p):
        return pl.ds(pl.multiple_of(p * slots_each, 16), slots_each)

    def exchange(src, dst, ss, rs):
        def out(d):
            p = lax.rem(me + d, ep_n)
            return remote(src.at[:, row_slots(p), :], dst.at[:, row_slots(me), :], ss.at[p], rs.at[me], g, p)

        def back(d):
            p = lax.rem(me + d, ep_n)
            return remote(src.at[:, row_slots(p), :], dst.at[:, row_slots(p), :], ss.at[p], rs.at[p], g, p)

        def start():
            lax.fori_loop(1, ep_n, lambda d, _: (out(d).start(), 0)[1], 0)
            dst[:, row_slots(me), :] = src[:, row_slots(me), :]

        def arrived():
            lax.fori_loop(1, ep_n, lambda d, _: (back(d).wait_recv(), 0)[1], 0)

        def sent():
            lax.fori_loop(1, ep_n, lambda d, _: (out(d).wait_send(), 0)[1], 0)

        return start, arrived, sent

    h_start, h_arrived, h_sent = exchange(h_send, h_recv, h_ss, h_rs)
    c_start, c_arrived, c_sent = exchange(c_send, c_recv, c_ss, c_rs)
    d_start, d_arrived, d_sent = exchange(d_send, d_recv, d_ss, d_rs)
    h_start()
    c_start()

    def gather(c):
        def step(s, _):
            from_left, from_right = g - 1 - s, g + 1 + s

            @pl.when(from_left >= 0)
            def _():
                landed(weight_copies(c, from_left, 0))
                pl.when(g < last)(lambda: go(weight_copies(c, from_left, 0)))

            @pl.when(from_right < grp_n)
            def _():
                landed(weight_copies(c, from_right, 1))
                pl.when(g > 0)(lambda: go(weight_copies(c, from_right, 1)))

            return 0

        lax.fori_loop(0, last, step, 0)

    def sum_copies(c, j, way):
        to = left if way else right
        lands = (right_up, right_down) if way else (left_up, left_down)
        return [
            remote(src.at[c, j], dst.at[c, j], rs_send.at[c, j, m], rs_recv.at[way, c, j, m], to, me)
            for m, (src, dst) in enumerate(zip((own_up, own_down), lands))
        ]

    def compute(c):
        pre_gate = jnp.zeros((slots, fc), F32)
        pre_up = jnp.zeros((slots, fc), F32)
        d_swiglu = jnp.zeros((slots, fc), F32)
        for j in range(grp_n):
            pre_gate += dot(h_recv[j], wgu_all[c, j, 0], 1, 0)
            pre_up += dot(h_recv[j], wgu_all[c, j, 1], 1, 0)
            d_swiglu += dot(c_recv[j], wd_all[c, j], 1, 1)
        sig = jax.nn.sigmoid(pre_gate)
        act = pre_gate * sig
        swiglu = (act * pre_up).astype(BF16)
        d_up = (d_swiglu * act).astype(BF16)
        gates[c] = (d_swiglu * pre_up * sig * (1.0 + pre_gate * (1.0 - sig))).astype(BF16)
        ups[c] = d_up

        def part(j):
            own_up[c, j] = dot(h_recv[j], d_up, 0, 0).astype(BF16)
            own_down[c, j] = dot(swiglu, c_recv[j], 0, 0).astype(BF16)

        def step(i, _):
            far = last - i

            @pl.when(g + far < grp_n)
            def _():
                part(g + far)
                pl.when(jnp.logical_and(g == 0, far > 0))(lambda: go(sum_copies(c, g + far, 0)))

            @pl.when(jnp.logical_and(g - far >= 0, far > 0))
            def _():
                part(g - far)
                pl.when(g == last)(lambda: go(sum_copies(c, g - far, 1)))

            return 0

        lax.fori_loop(0, grp_n, step, 0)

    def reduce(c):
        def add(j, lands):
            own_up[c, j] = (own_up[c, j].astype(F32) + lands[0][c, j].astype(F32)).astype(BF16)
            own_down[c, j] = (own_down[c, j].astype(F32) + lands[1][c, j].astype(F32)).astype(BF16)

        def step(i, _):
            far = last - i

            @pl.when(jnp.logical_and(g + far < grp_n, g > 0))
            def _():
                landed(sum_copies(c, g + far, 0))
                add(g + far, (left_up, left_down))
                go(sum_copies(c, g + far, 0))

            @pl.when(jnp.logical_and(g - far >= 0, g < last))
            def _():
                landed(sum_copies(c, g - far, 1))
                add(g - far, (right_up, right_down))
                go(sum_copies(c, g - far, 1))

            return 0

        lax.fori_loop(0, last, step, 0)
        cols = pl.ds(pl.multiple_of(c * fc, fc), fc)
        gu[:, cols] = own_up[c, g].astype(F32)
        gd[cols, :] = own_down[c, g].astype(F32)

        @pl.when(g > 0)
        def _():
            landed(sum_copies(c, g, 0))
            gu[:, cols] += left_up[c, g].astype(F32)
            gd[cols, :] += left_down[c, g].astype(F32)

        @pl.when(g < last)
        def _():
            landed(sum_copies(c, g, 1))
            gu[:, cols] += right_up[c, g].astype(F32)
            gd[cols, :] += right_down[c, g].astype(F32)

        gu[:, cols] *= factor
        gd[cols, :] *= factor

    def chunk(c, _):
        gather(c)
        pl.when(c + 2 < chunks)(lambda: own_shard(c + 2))

        @pl.when(c == 0)
        def _():
            h_arrived()
            c_arrived()

        compute(c)
        pl.when(c > 0)(lambda: reduce(c - 1))
        return 0

    lax.fori_loop(0, chunks, chunk, 0)

    def back_rows(j, _):
        total = jnp.zeros((slots, deep), F32)
        for c in range(chunks):
            total += dot(gates[c], wgu_all[c, j, 0], 1, 1)
            total += dot(ups[c], wgu_all[c, j, 1], 1, 1)
        d_send[j] = total.astype(BF16)
        return 0

    lax.fori_loop(0, grp_n, back_rows, 0)
    d_start()
    reduce(chunks - 1)
    d_arrived()

    pick = pick_s[...]
    inverse = inv_s[:, 0:1]
    mean = jnp.zeros((rows, 1), F32)
    scaled = []
    for j in range(grp_n):
        cols = slice(j * deep, (j + 1) * deep)
        s = dot(pick, d_recv[j], 0, 0) * gain[:, cols]
        mean += jnp.sum(s * normed_s[j], axis=1, keepdims=True)
        scaled.append(s)
    mean = mean * (1.0 / width)
    for j in range(grp_n):
        cols = slice(j * deep, (j + 1) * deep)
        gt[:, cols] = (inverse * (scaled[j] - normed_s[j] * mean)).astype(BF16)

    h_sent()
    c_sent()
    d_sent()

    def drain(i, _):
        c, j = i // grp_n, lax.rem(i, grp_n)
        pl.when(jnp.logical_and(j <= g, g < last))(lambda: gone(weight_copies(c, j, 0)))
        pl.when(jnp.logical_and(j >= g, g > 0))(lambda: gone(weight_copies(c, j, 1)))
        pl.when(j > g)(lambda: gone(sum_copies(c, j, 0)))
        pl.when(j < g)(lambda: gone(sum_copies(c, j, 1)))
        return 0

    lax.fori_loop(0, chunks * grp_n, drain, 0)


def shards(grp_n, ep_n, tokens, norm_gain, w_gate, w_up, w_down, expert_ids, probs, out_grad):
    rows, width = tokens.shape
    top = expert_ids.shape[1]
    inner = w_gate.shape[2]
    capacity = max(2, 3 * rows * top // (2 * ep_n))
    slots_each = -(-capacity // 16) * 16
    slots = ep_n * slots_each
    deep = width // grp_n
    chunks = inner // 128
    fc = inner // chunks
    factor = 1.0 / math.sqrt(rows * grp_n * ep_n * top / ep_n)
    dma = pltpu.SemaphoreType.DMA
    wide = [pltpu.VMEM((grp_n, slots, deep), BF16)] * 6
    ups, downs = pltpu.VMEM((chunks, grp_n, deep, fc), BF16), pltpu.VMEM((chunks, grp_n, fc, deep), BF16)
    vmem = pl.BlockSpec(memory_space=pltpu.VMEM)
    grad_tokens, grad_up, grad_down = pl.pallas_call(
        functools.partial(kernel, grp_n, ep_n, slots_each, chunks, factor),
        out_shape=(
            jax.ShapeDtypeStruct((rows, width), BF16),
            jax.ShapeDtypeStruct((deep, inner), F32),
            jax.ShapeDtypeStruct((inner, deep), F32),
        ),
        in_specs=[vmem] * 8,
        out_specs=(vmem, vmem, vmem),
        scratch_shapes=[
            pltpu.VMEM((chunks, grp_n, 2, deep, fc), BF16),
            downs,
            *wide,
            pltpu.VMEM((chunks, slots, fc), BF16),
            pltpu.VMEM((chunks, slots, fc), BF16),
            pltpu.VMEM((grp_n, rows, deep), F32),
            pltpu.VMEM((rows, 128), F32),
            pltpu.VMEM((slots, rows), BF16),
            ups, downs, ups, downs, ups, downs,
            dma((2, chunks, grp_n, 2)), dma((chunks, grp_n, 2)),
            dma((chunks, grp_n, 2)), dma((2, chunks, grp_n, 2)),
            dma((ep_n,)), dma((ep_n,)), dma((ep_n,)), dma((ep_n,)), dma((ep_n,)), dma((ep_n,)),
        ],
        compiler_params=pltpu.CompilerParams(
            collective_id=0, has_side_effects=True, vmem_limit_bytes=56 * 2**20
        ),
    )(
        tokens, norm_gain[None, :], w_gate[0], w_up[0], w_down[0], expert_ids.T, probs.T, out_grad,
    )
    return grad_tokens, grad_up[None], grad_down[None]


def solution(mesh):
    in_specs = (
        P(("grp", "ep"), None),
        P(),
        P("ep", "grp", None),
        P("ep", "grp", None),
        P("ep", None, "grp"),
        P(("grp", "ep"), None),
        P(("grp", "ep"), None),
        P(("grp", "ep"), None),
    )
    out_specs = (P(("grp", "ep"), None), P("ep", "grp", None), P("ep", None, "grp"))
    return jax.shard_map(
        functools.partial(shards, mesh.shape["grp"], mesh.shape["ep"]),
        mesh=mesh, in_specs=in_specs, out_specs=out_specs, check_vma=False,
    )
```

```python
import functools
import math

import jax
import jax.numpy as jnp
from jax import lax
from jax.experimental import pallas as pl
from jax.experimental.pallas import tpu as pltpu
from jax.sharding import PartitionSpec as P

EPS = 1e-06
F32 = jnp.float32
BF16 = jnp.bfloat16


def dot(a, b, ca, cb):
    return lax.dot_general(a, b, (((ca,), (cb,)), ((), ())), preferred_element_type=F32)


def kernel(
    grp_n, ep_n, slots_each, chunks, factor,
    tok, gain, wg, wu, wd, ids, probs, cot_in,
    gt, gu, gd,
    wgu_all, wd_all, h_send, c_send, h_recv, c_recv, d_send, d_recv,
    back_s, normed_s, inv_s, pick_s, own_up, own_down, left_up, left_down, right_up, right_down,
    ag_send, ag_recv, rs_send, rs_recv, h_ss, h_rs, c_ss, c_rs, d_ss, d_rs,
):
    g, me = lax.axis_index("grp"), lax.axis_index("ep")
    rows, width = tok.shape
    deep = width // grp_n
    fc = wg.shape[1] // chunks
    slots = ep_n * slots_each
    last = grp_n - 1
    right, left = lax.rem(g + 1, grp_n), lax.rem(g + grp_n - 1, grp_n)

    barrier = pltpu.get_barrier_semaphore()

    def greet(e_id, g_id):
        pl.semaphore_signal(
            barrier, inc=1, device_id=(g_id, e_id), device_id_type=pl.DeviceIdType.MESH
        )

    for d in range(1, ep_n):
        greet(lax.rem(me + d, ep_n), g)
    pl.when(g < last)(lambda: greet(me, right))
    pl.when(g > 0)(lambda: greet(me, left))
    beside = (g < last).astype(jnp.int32) + (g > 0).astype(jnp.int32)
    pl.semaphore_wait(barrier, ep_n - 1 + beside)

    def remote(src, dst, ss, rs, g_id, e_id):
        return pltpu.make_async_remote_copy(
            src_ref=src, dst_ref=dst, send_sem=ss, recv_sem=rs,
            device_id=(g_id, e_id), device_id_type=pl.DeviceIdType.MESH,
        )

    def weight_copies(c, j, way):
        to = left if way else right
        return [
            remote(buf.at[c, j], buf.at[c, j], ag_send.at[way, c, j, m], ag_recv.at[c, j, m], to, me)
            for m, buf in enumerate((wgu_all, wd_all))
        ]

    def go(copies):
        for copy in copies:
            copy.start()

    def landed(copies):
        for copy in copies:
            copy.wait_recv()

    def gone(copies):
        for copy in copies:
            copy.wait_send()

    def own_shard(c):
        pl.when(g < last)(lambda: go(weight_copies(c, g, 0)))
        pl.when(g > 0)(lambda: go(weight_copies(c, g, 1)))

    for c in range(chunks):
        cols = slice(c * fc, (c + 1) * fc)
        wgu_all[c, g, 0] = wg[:, cols]
        wgu_all[c, g, 1] = wu[:, cols]
        wd_all[c, g] = wd[cols, :]
        if c < 2:
            own_shard(c)

    id0, id1 = ids[0:1, :], ids[1:2, :]
    experts = lax.broadcasted_iota(jnp.int32, (ep_n, rows), 0)
    hit0, hit1 = (experts == id0).astype(F32), (experts == id1).astype(F32)
    before = lax.broadcasted_iota(jnp.int32, (rows, rows), 0) < lax.broadcasted_iota(
        jnp.int32, (rows, rows), 1
    )
    rank = dot((hit0 + hit1).astype(BF16), before.astype(F32).astype(BF16), 1, 0)
    at0 = id0 * slots_each + jnp.sum(hit0 * rank, axis=0, keepdims=True).astype(jnp.int32)
    at1 = id1 * slots_each + jnp.sum(hit1 * rank, axis=0, keepdims=True).astype(jnp.int32)
    slot = lax.broadcasted_iota(jnp.int32, (slots, rows), 0)
    pick0, pick1 = (slot == at0).astype(F32), (slot == at1).astype(F32)
    pick = (pick0 + pick1).astype(BF16)
    pick_s[...] = pick
    slot_prob = jnp.sum(pick0 * probs[0:1, :] + pick1 * probs[1:2, :], axis=1, keepdims=True)

    token_f = tok[...].astype(F32)
    inverse = lax.rsqrt(jnp.mean(token_f * token_f, axis=1, keepdims=True) + EPS)
    inv_s[...] = jnp.broadcast_to(inverse, inv_s.shape)
    for j in range(grp_n):
        cols = slice(j * deep, (j + 1) * deep)
        normed = tok[:, cols].astype(F32) * inverse
        normed_s[j] = normed
        hidden = (normed * gain[:, cols]).astype(BF16)
        h_send[j] = dot(pick, hidden, 1, 0).astype(BF16)
        c_send[j] = (dot(pick, cot_in[:, cols], 1, 0) * slot_prob).astype(BF16)

    def row_slots(p):
        return pl.ds(pl.multiple_of(p * slots_each, 16), slots_each)

    def exchange(src, dst, ss, rs):
        def out(d):
            p = lax.rem(me + d, ep_n)
            return remote(src.at[:, row_slots(p), :], dst.at[:, row_slots(me), :], ss.at[p], rs.at[me], g, p)

        def back(d):
            p = lax.rem(me + d, ep_n)
            return remote(src.at[:, row_slots(p), :], dst.at[:, row_slots(p), :], ss.at[p], rs.at[p], g, p)

        def start():
            lax.fori_loop(1, ep_n, lambda d, _: (out(d).start(), 0)[1], 0)
            dst[:, row_slots(me), :] = src[:, row_slots(me), :]

        def arrived():
            lax.fori_loop(1, ep_n, lambda d, _: (back(d).wait_recv(), 0)[1], 0)

        def sent():
            lax.fori_loop(1, ep_n, lambda d, _: (out(d).wait_send(), 0)[1], 0)

        return start, arrived, sent

    h_start, h_arrived, h_sent = exchange(h_send, h_recv, h_ss, h_rs)
    c_start, c_arrived, c_sent = exchange(c_send, c_recv, c_ss, c_rs)
    d_start, d_arrived, d_sent = exchange(d_send, d_recv, d_ss, d_rs)
    h_start()
    c_start()

    def gather(c):
        def step(s, _):
            from_left, from_right = g - 1 - s, g + 1 + s

            @pl.when(from_left >= 0)
            def _():
                landed(weight_copies(c, from_left, 0))
                pl.when(g < last)(lambda: go(weight_copies(c, from_left, 0)))

            @pl.when(from_right < grp_n)
            def _():
                landed(weight_copies(c, from_right, 1))
                pl.when(g > 0)(lambda: go(weight_copies(c, from_right, 1)))

            return 0

        lax.fori_loop(0, last, step, 0)

    def sum_copies(c, j, way):
        to = left if way else right
        lands = (right_up, right_down) if way else (left_up, left_down)
        return [
            remote(src.at[c, j], dst.at[c, j], rs_send.at[c, j, m], rs_recv.at[way, c, j, m], to, me)
            for m, (src, dst) in enumerate(zip((own_up, own_down), lands))
        ]

    def compute(c):
        pre_gate = jnp.zeros((slots, fc), F32)
        pre_up = jnp.zeros((slots, fc), F32)
        d_swiglu = jnp.zeros((slots, fc), F32)
        for j in range(grp_n):
            pre_gate += dot(h_recv[j], wgu_all[c, j, 0], 1, 0)
            pre_up += dot(h_recv[j], wgu_all[c, j, 1], 1, 0)
            d_swiglu += dot(c_recv[j], wd_all[c, j], 1, 1)
        sig = jax.nn.sigmoid(pre_gate)
        act = pre_gate * sig
        swiglu = (act * pre_up).astype(BF16)
        d_up = (d_swiglu * act).astype(BF16)
        d_gate = (d_swiglu * pre_up * sig * (1.0 + pre_gate * (1.0 - sig))).astype(BF16)

        def part(j):
            own_up[c, j] = dot(h_recv[j], d_up, 0, 0).astype(BF16)
            own_down[c, j] = dot(swiglu, c_recv[j], 0, 0).astype(BF16)

        def step(i, _):
            far = last - i

            @pl.when(g + far < grp_n)
            def _():
                part(g + far)
                pl.when(jnp.logical_and(g == 0, far > 0))(lambda: go(sum_copies(c, g + far, 0)))

            @pl.when(jnp.logical_and(g - far >= 0, far > 0))
            def _():
                part(g - far)
                pl.when(g == last)(lambda: go(sum_copies(c, g - far, 1)))

            return 0

        lax.fori_loop(0, grp_n, step, 0)

        def back_rows(first, final):
            for j in range(grp_n):
                total = dot(d_gate, wgu_all[c, j, 0], 1, 1) + dot(d_up, wgu_all[c, j, 1], 1, 1)
                if not first:
                    total += back_s[j]
                if final:
                    d_send[j] = total.astype(BF16)
                else:
                    back_s[j] = total

        if chunks == 1:
            back_rows(True, True)
        else:
            pl.when(c == 0)(lambda: back_rows(True, False))
            pl.when(jnp.logical_and(c > 0, c < chunks - 1))(lambda: back_rows(False, False))
            pl.when(c == chunks - 1)(lambda: back_rows(False, True))

    early = g >= (grp_n + 1) // 2

    def pass_on(c, way_is_left):
        def add(j, lands):
            own_up[c, j] = (own_up[c, j].astype(F32) + lands[0][c, j].astype(F32)).astype(BF16)
            own_down[c, j] = (own_down[c, j].astype(F32) + lands[1][c, j].astype(F32)).astype(BF16)

        def step(i, _):
            far = last - i

            go_right = jnp.logical_and(g + far < grp_n, g > 0)
            go_left = jnp.logical_and(g - far >= 0, g < last)

            @pl.when(jnp.logical_and(go_right, jnp.logical_not(way_is_left)))
            def _():
                landed(sum_copies(c, g + far, 0))
                add(g + far, (left_up, left_down))
                go(sum_copies(c, g + far, 0))

            @pl.when(jnp.logical_and(go_left, way_is_left))
            def _():
                landed(sum_copies(c, g - far, 1))
                add(g - far, (right_up, right_down))
                go(sum_copies(c, g - far, 1))

            return 0

        lax.fori_loop(0, last, step, 0)

    def finish(c, _):
        cols = pl.ds(pl.multiple_of(c * fc, fc), fc)
        up, down = own_up[c, g].astype(F32), own_down[c, g].astype(F32)

        @pl.when(g == 0)
        def _():
            landed(sum_copies(c, g, 1))
            gu[:, cols] = (up + right_up[c, g].astype(F32)) * factor
            gd[cols, :] = (down + right_down[c, g].astype(F32)) * factor

        @pl.when(g == last)
        def _():
            landed(sum_copies(c, g, 0))
            gu[:, cols] = (up + left_up[c, g].astype(F32)) * factor
            gd[cols, :] = (down + left_down[c, g].astype(F32)) * factor

        @pl.when(jnp.logical_and(g > 0, g < last))
        def _():
            landed(sum_copies(c, g, 0))
            landed(sum_copies(c, g, 1))
            sides = left_up[c, g].astype(F32) + right_up[c, g].astype(F32)
            gu[:, cols] = (up + sides) * factor
            sides = left_down[c, g].astype(F32) + right_down[c, g].astype(F32)
            gd[cols, :] = (down + sides) * factor

        return 0

    def chunk(c, _):
        gather(c)
        pl.when(c + 2 < chunks)(lambda: own_shard(c + 2))

        @pl.when(c == 0)
        def _():
            h_arrived()
            c_arrived()

        compute(c)
        pl.when(c > 0)(lambda: pass_on(c - 1, early))
        return 0

    lax.fori_loop(0, chunks, chunk, 0)

    d_start()

    def weights_left(i, _):
        c, j = i // grp_n, lax.rem(i, grp_n)
        right_near, left_near = jnp.logical_and(early, g < last), jnp.logical_and(jnp.logical_not(early), g > 0)
        pl.when(jnp.logical_and(j <= g, right_near))(lambda: gone(weight_copies(c, j, 0)))
        pl.when(jnp.logical_and(j >= g, left_near))(lambda: gone(weight_copies(c, j, 1)))
        return 0

    lax.fori_loop(0, chunks * grp_n, weights_left, 0)
    late = jnp.logical_not(early)
    lax.fori_loop(0, chunks - 1, lambda c, _: (pass_on(c, late), 0)[1], 0)
    pass_on(chunks - 1, early)
    pass_on(chunks - 1, late)
    lax.fori_loop(0, chunks - 1, finish, 0)
    d_arrived()

    pick = pick_s[...]
    inverse = inv_s[:, 0:1]
    mean = jnp.zeros((rows, 1), F32)
    scaled = []
    for j in range(grp_n):
        cols = slice(j * deep, (j + 1) * deep)
        s = dot(pick, d_recv[j], 0, 0) * gain[:, cols]
        mean += jnp.sum(s * normed_s[j], axis=1, keepdims=True)
        scaled.append(s)
    mean = mean * (1.0 / width)
    for j in range(grp_n):
        cols = slice(j * deep, (j + 1) * deep)
        gt[:, cols] = (inverse * (scaled[j] - normed_s[j] * mean)).astype(BF16)

    finish(chunks - 1, 0)

    h_sent()
    c_sent()
    d_sent()

    def drain(i, _):
        c, j = i // grp_n, lax.rem(i, grp_n)
        right_far, left_far = jnp.logical_and(late, g < last), jnp.logical_and(early, g > 0)
        pl.when(jnp.logical_and(j <= g, right_far))(lambda: gone(weight_copies(c, j, 0)))
        pl.when(jnp.logical_and(j >= g, left_far))(lambda: gone(weight_copies(c, j, 1)))
        pl.when(j > g)(lambda: gone(sum_copies(c, j, 0)))
        pl.when(j < g)(lambda: gone(sum_copies(c, j, 1)))
        return 0

    lax.fori_loop(0, chunks * grp_n, drain, 0)


def shards(grp_n, ep_n, tokens, norm_gain, w_gate, w_up, w_down, expert_ids, probs, out_grad):
    rows, width = tokens.shape
    top = expert_ids.shape[1]
    inner = w_gate.shape[2]
    capacity = max(2, 3 * rows * top // (2 * ep_n))
    slots_each = -(-capacity // 16) * 16
    slots = ep_n * slots_each
    deep = width // grp_n
    chunks = inner // 128
    fc = inner // chunks
    factor = 1.0 / math.sqrt(rows * grp_n * ep_n * top / ep_n)
    dma = pltpu.SemaphoreType.DMA
    wide = [pltpu.VMEM((grp_n, slots, deep), BF16)] * 6
    ups, downs = pltpu.VMEM((chunks, grp_n, deep, fc), BF16), pltpu.VMEM((chunks, grp_n, fc, deep), BF16)
    vmem = pl.BlockSpec(memory_space=pltpu.VMEM)
    grad_tokens, grad_up, grad_down = pl.pallas_call(
        functools.partial(kernel, grp_n, ep_n, slots_each, chunks, factor),
        out_shape=(
            jax.ShapeDtypeStruct((rows, width), BF16),
            jax.ShapeDtypeStruct((deep, inner), F32),
            jax.ShapeDtypeStruct((inner, deep), F32),
        ),
        in_specs=[vmem] * 8,
        out_specs=(vmem, vmem, vmem),
        scratch_shapes=[
            pltpu.VMEM((chunks, grp_n, 2, deep, fc), BF16),
            downs,
            *wide,
            pltpu.VMEM((grp_n, slots, deep), F32),
            pltpu.VMEM((grp_n, rows, deep), F32),
            pltpu.VMEM((rows, 128), F32),
            pltpu.VMEM((slots, rows), BF16),
            ups, downs, ups, downs, ups, downs,
            dma((2, chunks, grp_n, 2)), dma((chunks, grp_n, 2)),
            dma((chunks, grp_n, 2)), dma((2, chunks, grp_n, 2)),
            dma((ep_n,)), dma((ep_n,)), dma((ep_n,)), dma((ep_n,)), dma((ep_n,)), dma((ep_n,)),
        ],
        compiler_params=pltpu.CompilerParams(
            collective_id=0, has_side_effects=True, vmem_limit_bytes=56 * 2**20
        ),
    )(
        tokens, norm_gain[None, :], w_gate[0], w_up[0], w_down[0], expert_ids.T, probs.T, out_grad,
    )
    return grad_tokens, grad_up[None], grad_down[None]


def solution(mesh):
    in_specs = (
        P(("grp", "ep"), None),
        P(),
        P("ep", "grp", None),
        P("ep", "grp", None),
        P("ep", None, "grp"),
        P(("grp", "ep"), None),
        P(("grp", "ep"), None),
        P(("grp", "ep"), None),
    )
    out_specs = (P(("grp", "ep"), None), P("ep", "grp", None), P("ep", None, "grp"))
    return jax.shard_map(
        functools.partial(shards, mesh.shape["grp"], mesh.shape["ep"]),
        mesh=mesh, in_specs=in_specs, out_specs=out_specs, check_vma=False,
    )
```

```python
import functools
import math

import jax
import jax.numpy as jnp
from jax import lax
from jax.experimental import pallas as pl
from jax.experimental.pallas import tpu as pltpu
from jax.sharding import PartitionSpec as P

EPS = 1e-06
F32 = jnp.float32
BF16 = jnp.bfloat16


def dot(a, b, ca, cb):
    return lax.dot_general(a, b, (((ca,), (cb,)), ((), ())), preferred_element_type=F32)


def kernel(
    grp_n, ep_n, slots_each, chunks, factor,
    tok, gain, wg, wu, wd, ids, probs, cot_in,
    gt, gu, gd,
    wgu_all, wd_all, h_send, c_send, h_recv, c_recv, d_send, d_recv,
    back_s, normed_s, inv_s, pick_s, own_up, own_down, left_up, left_down, right_up, right_down,
    ag_send, ag_recv, rs_send, rs_recv, h_ss, h_rs, c_ss, c_rs, d_ss, d_rs,
):
    g, me = lax.axis_index("grp"), lax.axis_index("ep")
    rows, width = tok.shape
    deep = width // grp_n
    fc = wg.shape[1] // chunks
    slots = ep_n * slots_each
    last = grp_n - 1
    right, left = lax.rem(g + 1, grp_n), lax.rem(g + grp_n - 1, grp_n)

    barrier = pltpu.get_barrier_semaphore()

    def greet(e_id, g_id):
        pl.semaphore_signal(
            barrier, inc=1, device_id=(g_id, e_id), device_id_type=pl.DeviceIdType.MESH
        )

    for d in range(1, ep_n):
        greet(lax.rem(me + d, ep_n), g)
    pl.when(g < last)(lambda: greet(me, right))
    pl.when(g > 0)(lambda: greet(me, left))
    beside = (g < last).astype(jnp.int32) + (g > 0).astype(jnp.int32)
    pl.semaphore_wait(barrier, ep_n - 1 + beside)

    def remote(src, dst, ss, rs, g_id, e_id):
        return pltpu.make_async_remote_copy(
            src_ref=src, dst_ref=dst, send_sem=ss, recv_sem=rs,
            device_id=(g_id, e_id), device_id_type=pl.DeviceIdType.MESH,
        )

    def weight_copies(c, j, way):
        to = left if way else right
        return [
            remote(buf.at[c, j], buf.at[c, j], ag_send.at[way, c, j, m], ag_recv.at[c, j, m], to, me)
            for m, buf in enumerate((wgu_all, wd_all))
        ]

    def go(copies):
        for copy in copies:
            copy.start()

    def landed(copies):
        for copy in copies:
            copy.wait_recv()

    def gone(copies):
        for copy in copies:
            copy.wait_send()

    def own_shard(c):
        pl.when(g < last)(lambda: go(weight_copies(c, g, 0)))
        pl.when(g > 0)(lambda: go(weight_copies(c, g, 1)))

    for c in range(chunks):
        cols = slice(c * fc, (c + 1) * fc)
        wgu_all[c, g, 0] = wg[:, cols]
        wgu_all[c, g, 1] = wu[:, cols]
        wd_all[c, g] = wd[cols, :]
        if c < 3:
            own_shard(c)

    id0, id1 = ids[0:1, :], ids[1:2, :]
    experts = lax.broadcasted_iota(jnp.int32, (ep_n, rows), 0)
    hit0, hit1 = (experts == id0).astype(F32), (experts == id1).astype(F32)
    before = lax.broadcasted_iota(jnp.int32, (rows, rows), 0) < lax.broadcasted_iota(
        jnp.int32, (rows, rows), 1
    )
    rank = dot((hit0 + hit1).astype(BF16), before.astype(F32).astype(BF16), 1, 0)
    at0 = id0 * slots_each + jnp.sum(hit0 * rank, axis=0, keepdims=True).astype(jnp.int32)
    at1 = id1 * slots_each + jnp.sum(hit1 * rank, axis=0, keepdims=True).astype(jnp.int32)
    slot = lax.broadcasted_iota(jnp.int32, (slots, rows), 0)
    pick0, pick1 = (slot == at0).astype(F32), (slot == at1).astype(F32)
    pick = (pick0 + pick1).astype(BF16)
    pick_s[...] = pick
    slot_prob = jnp.sum(pick0 * probs[0:1, :] + pick1 * probs[1:2, :], axis=1, keepdims=True)

    token_f = tok[...].astype(F32)
    inverse = lax.rsqrt(jnp.mean(token_f * token_f, axis=1, keepdims=True) + EPS)
    inv_s[...] = jnp.broadcast_to(inverse, inv_s.shape)
    for j in range(grp_n):
        cols = slice(j * deep, (j + 1) * deep)
        normed = tok[:, cols].astype(F32) * inverse
        normed_s[j] = normed
        hidden = (normed * gain[:, cols]).astype(BF16)
        h_send[j] = dot(pick, hidden, 1, 0).astype(BF16)
        c_send[j] = (dot(pick, cot_in[:, cols], 1, 0) * slot_prob).astype(BF16)

    def row_slots(p):
        return pl.ds(pl.multiple_of(p * slots_each, 16), slots_each)

    def exchange(src, dst, ss, rs):
        def out(d):
            p = lax.rem(me + d, ep_n)
            return remote(src.at[:, row_slots(p), :], dst.at[:, row_slots(me), :], ss.at[p], rs.at[me], g, p)

        def back(d):
            p = lax.rem(me + d, ep_n)
            return remote(src.at[:, row_slots(p), :], dst.at[:, row_slots(p), :], ss.at[p], rs.at[p], g, p)

        def start():
            lax.fori_loop(1, ep_n, lambda d, _: (out(d).start(), 0)[1], 0)
            dst[:, row_slots(me), :] = src[:, row_slots(me), :]

        def arrived():
            lax.fori_loop(1, ep_n, lambda d, _: (back(d).wait_recv(), 0)[1], 0)

        def sent():
            lax.fori_loop(1, ep_n, lambda d, _: (out(d).wait_send(), 0)[1], 0)

        return start, arrived, sent

    h_start, h_arrived, h_sent = exchange(h_send, h_recv, h_ss, h_rs)
    c_start, c_arrived, c_sent = exchange(c_send, c_recv, c_ss, c_rs)
    d_start, d_arrived, d_sent = exchange(d_send, d_recv, d_ss, d_rs)
    h_start()
    c_start()

    def gather(c):
        def step(s, _):
            from_left, from_right = g - 1 - s, g + 1 + s

            @pl.when(from_left >= 0)
            def _():
                landed(weight_copies(c, from_left, 0))
                pl.when(g < last)(lambda: go(weight_copies(c, from_left, 0)))

            @pl.when(from_right < grp_n)
            def _():
                landed(weight_copies(c, from_right, 1))
                pl.when(g > 0)(lambda: go(weight_copies(c, from_right, 1)))

            return 0

        lax.fori_loop(0, last, step, 0)

    def sum_copies(c, j, way):
        to = left if way else right
        lands = (right_up, right_down) if way else (left_up, left_down)
        return [
            remote(src.at[c, j], dst.at[c, j], rs_send.at[c, j, m], rs_recv.at[way, c, j, m], to, me)
            for m, (src, dst) in enumerate(zip((own_up, own_down), lands))
        ]

    def compute(c):
        pre_gate = jnp.zeros((slots, fc), F32)
        pre_up = jnp.zeros((slots, fc), F32)
        d_swiglu = jnp.zeros((slots, fc), F32)
        for j in range(grp_n):
            pre_gate += dot(h_recv[j], wgu_all[c, j, 0], 1, 0)
            pre_up += dot(h_recv[j], wgu_all[c, j, 1], 1, 0)
            d_swiglu += dot(c_recv[j], wd_all[c, j], 1, 1)
        sig = jax.nn.sigmoid(pre_gate)
        act = pre_gate * sig
        swiglu = (act * pre_up).astype(BF16)
        d_up = (d_swiglu * act).astype(BF16)
        d_gate = (d_swiglu * pre_up * sig * (1.0 + pre_gate * (1.0 - sig))).astype(BF16)

        def part(j):
            own_up[c, j] = dot(h_recv[j], d_up, 0, 0).astype(BF16)
            own_down[c, j] = dot(swiglu, c_recv[j], 0, 0).astype(BF16)

        def step(i, _):
            far = last - i

            @pl.when(g + far < grp_n)
            def _():
                part(g + far)
                pl.when(jnp.logical_and(g == 0, far > 0))(lambda: go(sum_copies(c, g + far, 0)))

            @pl.when(jnp.logical_and(g - far >= 0, far > 0))
            def _():
                part(g - far)
                pl.when(g == last)(lambda: go(sum_copies(c, g - far, 1)))

            return 0

        lax.fori_loop(0, grp_n, step, 0)

        def back_rows(first, final):
            for j in range(grp_n):
                total = dot(d_gate, wgu_all[c, j, 0], 1, 1) + dot(d_up, wgu_all[c, j, 1], 1, 1)
                if not first:
                    total += back_s[j]
                if final:
                    d_send[j] = total.astype(BF16)
                else:
                    back_s[j] = total

        if chunks == 1:
            back_rows(True, True)
        else:
            pl.when(c == 0)(lambda: back_rows(True, False))
            pl.when(jnp.logical_and(c > 0, c < chunks - 1))(lambda: back_rows(False, False))
            pl.when(c == chunks - 1)(lambda: back_rows(False, True))

    early = g >= (grp_n + 1) // 2

    def pass_on(c, way_is_left):
        def add(j, lands):
            own_up[c, j] = (own_up[c, j].astype(F32) + lands[0][c, j].astype(F32)).astype(BF16)
            own_down[c, j] = (own_down[c, j].astype(F32) + lands[1][c, j].astype(F32)).astype(BF16)

        def step(i, _):
            far = last - i

            go_right = jnp.logical_and(g + far < grp_n, g > 0)
            go_left = jnp.logical_and(g - far >= 0, g < last)

            @pl.when(jnp.logical_and(go_right, jnp.logical_not(way_is_left)))
            def _():
                landed(sum_copies(c, g + far, 0))
                add(g + far, (left_up, left_down))
                go(sum_copies(c, g + far, 0))

            @pl.when(jnp.logical_and(go_left, way_is_left))
            def _():
                landed(sum_copies(c, g - far, 1))
                add(g - far, (right_up, right_down))
                go(sum_copies(c, g - far, 1))

            return 0

        lax.fori_loop(0, last, step, 0)

    def finish(c, _):
        cols = pl.ds(pl.multiple_of(c * fc, fc), fc)
        up, down = own_up[c, g].astype(F32), own_down[c, g].astype(F32)

        @pl.when(g == 0)
        def _():
            landed(sum_copies(c, g, 1))
            gu[:, cols] = (up + right_up[c, g].astype(F32)) * factor
            gd[cols, :] = (down + right_down[c, g].astype(F32)) * factor

        @pl.when(g == last)
        def _():
            landed(sum_copies(c, g, 0))
            gu[:, cols] = (up + left_up[c, g].astype(F32)) * factor
            gd[cols, :] = (down + left_down[c, g].astype(F32)) * factor

        @pl.when(jnp.logical_and(g > 0, g < last))
        def _():
            landed(sum_copies(c, g, 0))
            landed(sum_copies(c, g, 1))
            sides = left_up[c, g].astype(F32) + right_up[c, g].astype(F32)
            gu[:, cols] = (up + sides) * factor
            sides = left_down[c, g].astype(F32) + right_down[c, g].astype(F32)
            gd[cols, :] = (down + sides) * factor

        return 0

    inside = jnp.logical_and(g > 0, g < last)

    def chunk(c, _):
        pl.when(jnp.logical_or(c == 0, jnp.logical_not(inside)))(lambda: gather(c))
        pl.when(jnp.logical_and(c + 1 < chunks, inside))(lambda: gather(c + 1))
        pl.when(c + 3 < chunks)(lambda: own_shard(c + 3))

        @pl.when(c == 0)
        def _():
            h_arrived()
            c_arrived()

        compute(c)
        pl.when(c > 0)(lambda: pass_on(c - 1, early))
        return 0

    lax.fori_loop(0, chunks, chunk, 0)

    d_start()

    def weights_left(i, _):
        c, j = i // grp_n, lax.rem(i, grp_n)
        right_near, left_near = jnp.logical_and(early, g < last), jnp.logical_and(jnp.logical_not(early), g > 0)
        pl.when(jnp.logical_and(j <= g, right_near))(lambda: gone(weight_copies(c, j, 0)))
        pl.when(jnp.logical_and(j >= g, left_near))(lambda: gone(weight_copies(c, j, 1)))
        return 0

    lax.fori_loop(0, chunks * grp_n, weights_left, 0)
    late = jnp.logical_not(early)
    lax.fori_loop(0, chunks - 1, lambda c, _: (pass_on(c, late), 0)[1], 0)
    pass_on(chunks - 1, early)
    pass_on(chunks - 1, late)
    lax.fori_loop(0, chunks - 1, finish, 0)
    d_arrived()

    pick = pick_s[...]
    inverse = inv_s[:, 0:1]
    mean = jnp.zeros((rows, 1), F32)
    scaled = []
    for j in range(grp_n):
        cols = slice(j * deep, (j + 1) * deep)
        s = dot(pick, d_recv[j], 0, 0) * gain[:, cols]
        mean += jnp.sum(s * normed_s[j], axis=1, keepdims=True)
        scaled.append(s)
    mean = mean * (1.0 / width)
    for j in range(grp_n):
        cols = slice(j * deep, (j + 1) * deep)
        gt[:, cols] = (inverse * (scaled[j] - normed_s[j] * mean)).astype(BF16)

    finish(chunks - 1, 0)

    h_sent()
    c_sent()
    d_sent()

    def drain(i, _):
        c, j = i // grp_n, lax.rem(i, grp_n)
        right_far, left_far = jnp.logical_and(late, g < last), jnp.logical_and(early, g > 0)
        pl.when(jnp.logical_and(j <= g, right_far))(lambda: gone(weight_copies(c, j, 0)))
        pl.when(jnp.logical_and(j >= g, left_far))(lambda: gone(weight_copies(c, j, 1)))
        pl.when(j > g)(lambda: gone(sum_copies(c, j, 0)))
        pl.when(j < g)(lambda: gone(sum_copies(c, j, 1)))
        return 0

    lax.fori_loop(0, chunks * grp_n, drain, 0)


def shards(grp_n, ep_n, tokens, norm_gain, w_gate, w_up, w_down, expert_ids, probs, out_grad):
    rows, width = tokens.shape
    top = expert_ids.shape[1]
    inner = w_gate.shape[2]
    capacity = max(2, 3 * rows * top // (2 * ep_n))
    slots_each = -(-capacity // 16) * 16
    slots = ep_n * slots_each
    deep = width // grp_n
    chunks = inner // 128
    fc = inner // chunks
    factor = 1.0 / math.sqrt(rows * grp_n * ep_n * top / ep_n)
    dma = pltpu.SemaphoreType.DMA
    wide = [pltpu.VMEM((grp_n, slots, deep), BF16)] * 6
    ups, downs = pltpu.VMEM((chunks, grp_n, deep, fc), BF16), pltpu.VMEM((chunks, grp_n, fc, deep), BF16)
    vmem = pl.BlockSpec(memory_space=pltpu.VMEM)
    grad_tokens, grad_up, grad_down = pl.pallas_call(
        functools.partial(kernel, grp_n, ep_n, slots_each, chunks, factor),
        out_shape=(
            jax.ShapeDtypeStruct((rows, width), BF16),
            jax.ShapeDtypeStruct((deep, inner), F32),
            jax.ShapeDtypeStruct((inner, deep), F32),
        ),
        in_specs=[vmem] * 8,
        out_specs=(vmem, vmem, vmem),
        scratch_shapes=[
            pltpu.VMEM((chunks, grp_n, 2, deep, fc), BF16),
            downs,
            *wide,
            pltpu.VMEM((grp_n, slots, deep), F32),
            pltpu.VMEM((grp_n, rows, deep), F32),
            pltpu.VMEM((rows, 128), F32),
            pltpu.VMEM((slots, rows), BF16),
            ups, downs, ups, downs, ups, downs,
            dma((2, chunks, grp_n, 2)), dma((chunks, grp_n, 2)),
            dma((chunks, grp_n, 2)), dma((2, chunks, grp_n, 2)),
            dma((ep_n,)), dma((ep_n,)), dma((ep_n,)), dma((ep_n,)), dma((ep_n,)), dma((ep_n,)),
        ],
        compiler_params=pltpu.CompilerParams(
            collective_id=0, has_side_effects=True, vmem_limit_bytes=56 * 2**20
        ),
    )(
        tokens, norm_gain[None, :], w_gate[0], w_up[0], w_down[0], expert_ids.T, probs.T, out_grad,
    )
    return grad_tokens, grad_up[None], grad_down[None]


def solution(mesh):
    in_specs = (
        P(("grp", "ep"), None),
        P(),
        P("ep", "grp", None),
        P("ep", "grp", None),
        P("ep", None, "grp"),
        P(("grp", "ep"), None),
        P(("grp", "ep"), None),
        P(("grp", "ep"), None),
    )
    out_specs = (P(("grp", "ep"), None), P("ep", "grp", None), P("ep", None, "grp"))
    return jax.shard_map(
        functools.partial(shards, mesh.shape["grp"], mesh.shape["ep"]),
        mesh=mesh, in_specs=in_specs, out_specs=out_specs, check_vma=False,
    )
```
